32 devices in a mesh: row: 8 (over y, x, core), col: 4 (over z).
Axes of the slice: x: 2, y: 2, z: 4, core: 2. Of those that a mesh axis runs over, the one named last changes fastest.
Arguments:
- spectra: bfloat16 [16384, 4096], P(('row', 'col')), may hold values from 0 to 16, as said below
- projection: bfloat16 [4096, 1024], replicated, may hold values from -0.09375 to 0.09375
- kernel_slot: int32 [16384], P(('row', 'col')), may hold values from 0 to 16383, as said below
- env_image: int32 [16384], P(('row', 'col')), may hold values from 0 to 1023, never falling along the last dimension, each value on 1 to 48 neighbouring positions
- image_atoms: int32 [1024], replicated, may hold values from 8 to 64
Outputs:
- panels: float32 [16384, 1024], P('row')
- trailing: float32 [16384, 16384], P('row', 'col')
The draws below stay inside these ranges and needn't reach their ends.
Inputs may be any that keep to these rules, and one draw needn't show every extreme that they name: `spectra`: Nonnegative. A permutation. With the block of environment e being kernel_slot[e] // 512: among the 512 environments of one device (aligned blocks of 512 in environment order) at most 16 fall in any one block, and in every draw some block receives 16 of them.
All inputs are finite; a program needn't handle non-finite values.
Results may differ from the reference program's by a relative error of at most 0.0063.
Values may be sent and summed in bfloat16 or wider, within the bound.
A program may use at most 192 MiB of HBM per device.

```python
import math
import jax
import jax.numpy as jnp
import numpy as np
from jax import lax

M = 16384
Q = 4096
K = 1024
NB = 512
PANELS = 2
IMAGES = 1024
MOST = 48
PROW = 8
PCOL = 4
GRID = 32
PER = 512
ROW_GROUP = 2048


def draw_spectra(key, part):
    key_rows, key_cols, key_base = jax.random.split(key, 3)
    row_scale = jnp.exp(jax.random.uniform(key_rows, (M, 1), jnp.float32, 0.0, math.log(10.0)))
    base_values = jax.random.uniform(key_base, (M, Q), jnp.float32)
    col_scale = jnp.exp(jax.random.uniform(key_cols, (1, Q), jnp.float32, math.log(0.1), 0.0))
    return (row_scale * col_scale * base_values).astype(jnp.bfloat16)


def random_ranks(key, shape_rows, shape_cols):
    scores = jax.random.randint(key, (shape_rows, shape_cols), 0, 1 << 20) * shape_cols + jnp.arange(shape_cols, dtype=jnp.int32)[None, :]
    return jnp.argsort(jnp.argsort(scores, axis=1), axis=1).astype(jnp.int32)


def draw_kernel_slot(key, part):
    key_order, key_devices, key_inner = jax.random.split(jax.random.fold_in(key, 7), 3)
    order = random_ranks(key_order, GRID, PER)
    devices_perm = jax.random.permutation(key_devices, GRID).astype(jnp.int32)
    values = order * GRID + devices_perm[:, None]
    blocks = values // PER
    shuffle = random_ranks(key_inner, GRID, PER)
    inner = shuffle[blocks, values % PER]
    return (blocks * PER + inner).reshape(-1).astype(jnp.int32)


def place_ends(result, stream_key, low, high):
    shape = result.shape
    spot = [jax.random.randint(jax.random.fold_in(stream_key, axis), (), 0, shape[axis]) for axis in range(len(shape))]
    result = result.at[tuple(spot)].set(low)
    longest = shape.index(max(shape))
    spot[longest] = (spot[longest] + 1) % shape[longest]
    return result.at[tuple(spot)].set(high)


def length_profile(amount, total, most, skew):
    weights = [(1 << 20) // math.isqrt(grade ** skew) + 1 for grade in range(2, amount + 1)]
    surplus, given = total - most - (amount - 1), [1] * (amount - 1)
    while surplus > 0:
        candidates = [i for i in range(amount - 1) if given[i] < most]
        whole, remaining = sum([weights[i] for i in candidates]), surplus
        for i in candidates:
            addition = min(most - given[i], max(1, remaining * weights[i] // whole), surplus)
            given[i] = given[i] + addition
            surplus = surplus - addition
    return np.array([most] + given)


def uneven(rng, amount, total, bound, skew):
    if amount == 2:
        one = jax.random.randint(rng, (), max(1, total - bound), min(bound, total - 1) + 1)
        return jnp.stack([one, total - one])
    tallies = jnp.asarray(length_profile(amount, total, bound, skew), jnp.int32)
    pairs = (amount - 1) // 2
    giver, sink = tallies[1:1 + 2 * pairs:2], tallies[2:2 + 2 * pairs:2]
    margin = jnp.minimum(giver - 1, bound - sink)
    passed = jax.random.randint(jax.random.fold_in(rng, 1), (pairs,), 0, 1 << 20) % (margin + 1)
    tallies = tallies.at[1:1 + 2 * pairs:2].set(giver - passed).at[2:2 + 2 * pairs:2].set(sink + passed)
    return tallies[jax.random.permutation(jax.random.fold_in(rng, 2), amount)]


def normal_values(stream_key, shape, width, reach, held_as=jnp.bfloat16):
    return jnp.clip(width * jax.random.normal(stream_key, shape, jnp.float32), -reach, reach).astype(held_as)


def setup_inputs(seed: int = 0) -> dict:
    keys = jax.random.split(jax.random.key(seed), 6)
    spectra = draw_spectra(jax.random.fold_in(keys[5], 71), 0)
    projection = normal_values(keys[1], (Q, K), Q ** -0.5, 0.09375)
    kernel_slot = draw_kernel_slot(jax.random.fold_in(keys[5], 71), 0)
    env_image = jnp.searchsorted(jnp.cumsum(uneven(keys[3], IMAGES, M, MOST, 2)), jnp.arange(M), side="right").astype(jnp.int32)
    image_atoms = place_ends(jax.random.randint(keys[4], (IMAGES,), 8, 65), jax.random.fold_in(keys[4], 1), 8, 64).astype(jnp.int32)
    return dict(spectra=spectra, projection=projection, kernel_slot=kernel_slot, env_image=env_image, image_atoms=image_atoms)


ATOM_RIDGE = 0.02
NORM_EPS = 1e-06

def reference(spectra, projection, kernel_slot, env_image, image_atoms):
    projected = jnp.dot(spectra.astype(jnp.float32), projection.astype(jnp.float32), preferred_element_type=jnp.float32)
    factor = lax.rsqrt(lax.optimization_barrier(jnp.mean(projected * projected, axis=1, keepdims=True)) + NORM_EPS) * K ** (-0.5)
    unit_rows = (projected * factor).astype(jnp.bfloat16)
    stored = jnp.zeros((M, K), jnp.bfloat16).at[kernel_slot].set(unit_rows)
    ridge_env = ATOM_RIDGE * jnp.take(image_atoms, env_image).astype(jnp.float32)
    ridge_diag = jnp.zeros((M,), jnp.float32).at[kernel_slot].set(ridge_env)
    gram_matrix = jnp.dot(stored.astype(jnp.float32), stored.T.astype(jnp.float32), preferred_element_type=jnp.float32)
    positions = jnp.arange(M, dtype=jnp.int32)
    covariance = (gram_matrix * gram_matrix).at[positions, positions].add(ridge_diag)
    tile_of = positions % ROW_GROUP // NB * PROW + positions // ROW_GROUP
    panel_list = []
    for panel_index in range(PANELS):
        pivot_start = panel_index % PROW * ROW_GROUP + panel_index // PROW * NB
        lower_factor = jnp.linalg.cholesky(covariance[pivot_start:pivot_start + NB, pivot_start:pivot_start + NB])
        solved = lax.linalg.triangular_solve(lower_factor, covariance[:, pivot_start:pivot_start + NB], left_side=False, lower=True, transpose_a=True)
        solved = jnp.where((tile_of >= panel_index)[:, None], solved, 0.0)
        covariance = covariance - jnp.dot(solved.astype(jnp.float32), solved.T.astype(jnp.float32), precision=lax.Precision.HIGHEST, preferred_element_type=jnp.float32)
        panel_list.append(solved)
    panels = jnp.concatenate(panel_list, axis=1)
    trailing = covariance.reshape(M, PROW // PCOL, PCOL, ROW_GROUP).transpose(0, 2, 1, 3).reshape(M, M)
    return (panels, trailing)
```

```python
import functools

import jax
import jax.numpy as jnp
from jax import lax
from jax.experimental import pallas as pl
from jax.experimental.pallas import tpu as pltpu
from jax.sharding import PartitionSpec as P

NB = 512
PANELS = 2
ATOM_RIDGE = 0.02
NORM_EPS = 1e-06

LANES = 128
META_ROWS = 16
DIGIT = 256
HIGHEST = lax.Precision.HIGHEST
HIGH = lax.Precision.HIGH


def column_owner(blocks, grid_cols):
    group_row = blocks // grid_cols
    target_row = group_row // grid_cols * grid_cols + blocks % grid_cols
    return target_row * grid_cols + group_row % grid_cols


def one_hot(rows, positions):
    ids = lax.broadcasted_iota(jnp.int32, (rows, positions.shape[0]), 0)
    return (ids == positions[None, :]).astype(jnp.bfloat16)


def pick(selector, values):
    return jnp.dot(selector, values, preferred_element_type=jnp.float32).astype(jnp.bfloat16)


def slots_of(meta):
    digits = meta[:, :2].astype(jnp.int32)
    return digits[:, 0] * DIGIT + digits[:, 1]


def factor_kernel(a_ref, inv_ref, work_ref, diag_ref):
    n = a_ref.shape[0]
    count = n // LANES
    groups = LANES // 8
    work_ref[:, :n] = a_ref[...]
    work_ref[:, n:] = jnp.zeros((n, n), jnp.float32)
    row_ids = lax.broadcasted_iota(jnp.int32, (LANES, LANES), 0)
    col_ids = lax.broadcasted_iota(jnp.int32, (LANES, LANES), 1)
    eye = jnp.where(row_ids == col_ids, 1.0, 0.0).astype(jnp.float32)

    def step(block, carry):
        start = pl.multiple_of(block * LANES, LANES)
        rows = pl.ds(start, LANES)
        tile = work_ref[rows, rows]
        left = [tile[8 * g : 8 * g + 8, :] for g in range(groups)]
        right = [eye[8 * g : 8 * g + 8, :] for g in range(groups)]
        for k in range(LANES):
            g, s = k // 8, k % 8
            scale = lax.rsqrt(left[g][s : s + 1, k : k + 1])
            left_row = left[g][s : s + 1, :] * scale
            right_row = right[g][s : s + 1, :] * scale
            diag_ref[k : k + 1, :] = right_row
            for h in range(g if s < 7 else g + 1, groups):
                column = left[h][:, k : k + 1] * scale
                left[h] = left[h] - column * left_row
                right[h] = right[h] - column * right_row
        inverse = diag_ref[...]
        work_ref[rows, pl.ds(pl.multiple_of(n + start, LANES), LANES)] = eye
        window = pl.ds(pl.multiple_of(start + LANES, LANES), n)
        solved = jnp.dot(inverse, work_ref[rows, window], precision=HIGHEST, preferred_element_type=jnp.float32)
        work_ref[rows, window] = solved

        def below(other, inner):
            other_rows = pl.ds(pl.multiple_of(other * LANES, LANES), LANES)
            lower = work_ref[rows, other_rows]
            work_ref[other_rows, window] = work_ref[other_rows, window] - lax.dot_general(
                lower,
                work_ref[rows, window],
                (((0,), (0,)), ((), ())),
                precision=HIGHEST,
                preferred_element_type=jnp.float32,
            )
            return inner

        lax.fori_loop(block + 1, count, below, 0)
        return carry

    lax.fori_loop(0, count, step, 0)
    inv_ref[...] = work_ref[:, n:]


def inverse_factor(matrix):
    n = matrix.shape[0]
    return pl.pallas_call(
        factor_kernel,
        out_shape=jax.ShapeDtypeStruct((n, n), jnp.float32),
        in_specs=[pl.BlockSpec(memory_space=pltpu.VMEM)],
        out_specs=pl.BlockSpec(memory_space=pltpu.VMEM),
        scratch_shapes=[pltpu.VMEM((n, 2 * n), jnp.float32), pltpu.VMEM((LANES, LANES), jnp.float32)],
        compiler_params=pltpu.CompilerParams(vmem_limit_bytes=40 * 1024 * 1024),
        cost_estimate=pl.CostEstimate(flops=120 * 10**9, bytes_accessed=8 * n * n, transcendentals=0),
    )(matrix)


def trailing_kernel(
    chunk, place_ref, rows_ref, weights_ref, sums_ref, ridge_ref, pivots_ref, pivot_ridge_ref, pivot_ids_ref, cols_ref, out_ref
):
    width = cols_ref.shape[0]
    row_base = place_ref[0]
    row_group = place_ref[2]
    start = pl.program_id(0) * width
    group = start // row_group
    col_base = (place_ref[1] + group * place_ref[3]) * row_group + start - group * row_group
    cols = cols_ref[...]
    col_ids = col_base + lax.broadcasted_iota(jnp.int32, (1, width), 1)
    gram = lax.dot_general(pivots_ref[...], cols, (((1,), (1,)), ((), ())), preferred_element_type=jnp.float32)
    cross = gram * gram + jnp.where(pivot_ids_ref[...] == col_ids, pivot_ridge_ref[...], 0.0)
    centre = jnp.mean(cross, axis=0, keepdims=True)
    spread = (cross - centre).astype(jnp.bfloat16)
    for first in range(0, rows_ref.shape[0], chunk):
        part = pl.ds(first, chunk)
        gram = lax.dot_general(rows_ref[part, :], cols, (((1,), (1,)), ((), ())), preferred_element_type=jnp.float32)
        update = jnp.dot(weights_ref[part, :], spread, preferred_element_type=jnp.float32)
        row_ids = row_base + first + lax.broadcasted_iota(jnp.int32, (chunk, 1), 0)
        ridge = jnp.where(row_ids == col_ids, ridge_ref[part, :], 0.0)
        out_ref[part, :] = gram * gram + ridge - (update + sums_ref[part, :] * centre)


def trailing_update(place, rows, weights, sums, ridge, pivots, pivot_ridge, pivot_ids, cols):
    row_group, depth = rows.shape
    col_group = cols.shape[0]
    width = min(512, row_group)
    chunk = min(512, row_group)
    held = pl.BlockSpec(memory_space=pltpu.VMEM)
    return pl.pallas_call(
        functools.partial(trailing_kernel, chunk),
        out_shape=jax.ShapeDtypeStruct((row_group, col_group), jnp.float32),
        grid=(col_group // width,),
        in_specs=[pl.BlockSpec(memory_space=pltpu.SMEM)]
        + [held] * 7
        + [pl.BlockSpec((width, depth), lambda j: (j, 0))],
        out_specs=pl.BlockSpec((row_group, width), lambda j: (0, j)),
        compiler_params=pltpu.CompilerParams(
            dimension_semantics=("arbitrary",), vmem_limit_bytes=52 * 1024 * 1024
        ),
        cost_estimate=pl.CostEstimate(
            flops=4 * row_group * col_group * depth,
            bytes_accessed=4 * row_group * col_group + 2 * depth * (2 * row_group + col_group),
            transcendentals=0,
        ),
    )(place, rows, weights, sums, ridge, pivots, pivot_ridge, pivot_ids, cols)


def gather_blocks(block, axis):
    count = lax.axis_size(axis)
    index = lax.axis_index(axis)
    arrived = [block]
    for shift in range(1, count):
        if count & (count - 1) == 0:
            pairs = [(i, i ^ shift) for i in range(count)]
        else:
            pairs = [(i, (i + shift) % count) for i in range(count)]
        arrived.append(lax.ppermute(block, axis, pairs))

    def place(arrived):
        result = jnp.zeros((count,) + block.shape, block.dtype)
        for shift, part in enumerate(arrived):
            source = (index ^ shift) if count & (count - 1) == 0 else (index - shift) % count
            result = lax.dynamic_update_slice(result, part[None], (source, 0, 0))
        return result

    return arrived, place


def body(spectra, projection, kernel_slot, env_image, image_atoms):
    grid_rows = lax.axis_size("row")
    grid_cols = lax.axis_size("col")
    devices = grid_rows * grid_cols
    per_device = spectra.shape[0]
    total_rows = per_device * devices
    depth = projection.shape[1]
    row_group = total_rows // grid_rows
    capacity = max(1, per_device // devices)
    share = NB // devices
    row_index = lax.axis_index("row")
    col_index = lax.axis_index("col")

    projected = jnp.dot(spectra, projection, preferred_element_type=jnp.float32)
    factor = lax.rsqrt(jnp.mean(projected * projected, axis=1, keepdims=True) + NORM_EPS) * depth ** (-0.5)
    unit_rows = (projected * factor).astype(jnp.bfloat16)

    image_ids = jnp.arange(image_atoms.shape[0], dtype=jnp.int32)
    atoms = jnp.sum(jnp.where(env_image[:, None] == image_ids[None, :], image_atoms[None, :], 0), axis=1)
    meta = jnp.stack([kernel_slot // DIGIT, kernel_slot % DIGIT, atoms], axis=1).astype(jnp.bfloat16)
    meta = jnp.pad(meta, ((0, 0), (0, LANES - meta.shape[1])))
    rows_out = jnp.concatenate([unit_rows, meta], axis=1)

    positions = jnp.arange(per_device, dtype=jnp.int32)
    before = positions[None, :] < positions[:, None]

    def rank_of(label):
        return jnp.sum(((label[:, None] == label[None, :]) & before).astype(jnp.int32), axis=1)

    starts = [j % grid_rows * row_group + j // grid_rows * NB for j in range(PANELS)]
    tile = kernel_slot // NB
    tile_rank = rank_of(tile)
    pivot_place = jnp.full((per_device,), -1, jnp.int32)
    for j, first in enumerate(starts):
        pivot_place = jnp.where(tile == first // NB, j * share + tile_rank, pivot_place)
    pivot_sent = pick(one_hot(PANELS * share, pivot_place), rows_out)
    pivot_all = lax.all_gather(pivot_sent, ("row", "col"), axis=0, tiled=True)
    pivot_slot = slots_of(pivot_all[:, depth:])
    pivot_order = jnp.full((PANELS * NB,), -1, jnp.int32)
    for j, first in enumerate(starts):
        pivot_order = jnp.where(pivot_slot // NB == first // NB, j * NB + pivot_slot - first, pivot_order)
    pivot_rows = pick(one_hot(PANELS * NB, pivot_order), pivot_all)
    pivots = pivot_rows[:, :depth]
    pivot_ridge = ATOM_RIDGE * pivot_rows[:, depth + 2].astype(jnp.float32)
    pivot_ids = jnp.concatenate([first + jnp.arange(NB, dtype=jnp.int32) for first in starts])
    pivot_gram = lax.dot_general(pivots, pivots, (((1,), (1,)), ((), ())), preferred_element_type=jnp.float32)
    pivot_matrix = pivot_gram * pivot_gram + jnp.where(
        pivot_ids[:, None] == pivot_ids[None, :], pivot_ridge[:, None], 0.0
    )

    block = kernel_slot // per_device
    rank = rank_of(block)
    row_place = block * (2 * capacity) + rank
    col_place = column_owner(block, grid_cols) * (2 * capacity) + capacity + rank
    ids = lax.broadcasted_iota(jnp.int32, (2 * per_device, per_device), 0)
    selector = ((ids == row_place[None, :]) | (ids == col_place[None, :])).astype(jnp.bfloat16)
    sent = pick(selector, rows_out)
    received = lax.all_to_all(sent, ("row", "col"), split_axis=0, concat_axis=0, tiled=True)
    received = received.reshape(devices, 2, capacity, rows_out.shape[1])
    for_rows = received[:, 0].reshape(per_device, -1)
    for_cols = received[:, 1].reshape(per_device, -1)
    row_selector = one_hot(per_device, slots_of(for_rows[:, depth:]) % per_device)
    col_selector = one_hot(per_device, slots_of(for_cols[:, depth:]) % per_device)
    own_rows = pick(row_selector, for_rows[:, :depth])
    own_cols = pick(col_selector, for_cols[:, :depth])
    own_meta = lax.dot_general(
        for_rows[:, depth:], row_selector, (((0,), (1,)), ((), ())), preferred_element_type=jnp.float32
    ).astype(jnp.bfloat16)
    own_meta = jnp.pad(own_meta[:META_ROWS], ((0, 0), (0, depth - per_device)))
    own_block = jnp.concatenate([own_rows, own_meta], axis=0)

    row_parts, place_rows = gather_blocks(own_block, "col")
    col_parts, place_cols = gather_blocks(own_cols, "row")
    inverse = inverse_factor(pivot_matrix)
    inverse, row_parts, col_parts = lax.optimization_barrier((inverse, row_parts, col_parts))
    row_blocks = place_rows(row_parts)
    cols = place_cols(col_parts).reshape(grid_rows * per_device, depth)
    rows = row_blocks[:, :per_device].reshape(row_group, depth)
    ridge = ATOM_RIDGE * row_blocks[:, per_device + 2, :per_device].reshape(row_group).astype(jnp.float32)

    row_positions = jnp.arange(row_group, dtype=jnp.int32)
    row_ids = row_index * row_group + row_positions
    gram = lax.dot_general(rows, pivots, (((1,), (1,)), ((), ())), preferred_element_type=jnp.float32)
    cross = gram * gram + jnp.where(row_ids[:, None] == pivot_ids[None, :], pivot_ridge[None, :], 0.0)
    panels = lax.dot_general(cross, inverse, (((1,), (1,)), ((), ())), precision=HIGH, preferred_element_type=jnp.float32)
    row_tile = row_positions // NB * grid_rows + row_index
    panel_of = jnp.arange(PANELS * NB, dtype=jnp.int32) // NB
    panels = jnp.where(row_tile[:, None] >= panel_of[None, :], panels, 0.0)
    weights = jnp.dot(panels, inverse, precision=HIGH, preferred_element_type=jnp.float32)
    place = jnp.stack([row_index * row_group, col_index, jnp.int32(row_group), jnp.int32(grid_cols)]).astype(jnp.int32)
    trailing = trailing_update(
        place,
        rows,
        weights.astype(jnp.bfloat16),
        jnp.sum(weights, axis=1, keepdims=True),
        ridge[:, None],
        pivots,
        pivot_ridge[:, None],
        pivot_ids[:, None],
        cols,
    )
    return (panels, trailing)


def solution(mesh):
    in_specs = (P(("row", "col"), None), P(), P(("row", "col")), P(("row", "col")), P())
    out_specs = (P("row", None), P("row", "col"))
    return jax.shard_map(body, mesh=mesh, in_specs=in_specs, out_specs=out_specs, check_vma=False)
```

```python
import functools

import jax
import jax.numpy as jnp
from jax import lax
from jax.experimental import pallas as pl
from jax.experimental.pallas import tpu as pltpu
from jax.sharding import PartitionSpec as P

NB = 512
PANELS = 2
ATOM_RIDGE = 0.02
NORM_EPS = 1e-06

LANES = 128
META_ROWS = 16
DIGIT = 256
HIGHEST = lax.Precision.HIGHEST
HIGH = lax.Precision.HIGH


def column_owner(blocks, grid_cols):
    group_row = blocks // grid_cols
    target_row = group_row // grid_cols * grid_cols + blocks % grid_cols
    return target_row * grid_cols + group_row % grid_cols


def one_hot(rows, positions):
    ids = lax.broadcasted_iota(jnp.int32, (rows, positions.shape[0]), 0)
    return (ids == positions[None, :]).astype(jnp.bfloat16)


def pick(selector, values):
    return jnp.dot(selector, values, preferred_element_type=jnp.float32).astype(jnp.bfloat16)


def slots_of(meta):
    digits = meta[:, :2].astype(jnp.int32)
    return digits[:, 0] * DIGIT + digits[:, 1]


def first_blocks_kernel(stop, a_ref, work_ref, diag_ref):
    n = a_ref.shape[0]
    work_ref[:, :n] = a_ref[...]
    work_ref[:, n:] = jnp.zeros((n, n), jnp.float32)
    eliminate(0, stop, work_ref, diag_ref)


def last_blocks_kernel(start, state_ref, inv_ref, work_ref, diag_ref):
    n = inv_ref.shape[0]
    work_ref[...] = state_ref[...]
    eliminate(start, n // LANES, work_ref, diag_ref)
    inv_ref[...] = work_ref[:, n:]


def eliminate(begin, end, work_ref, diag_ref):
    n = work_ref.shape[0]
    count = n // LANES
    groups = LANES // 8
    row_ids = lax.broadcasted_iota(jnp.int32, (LANES, LANES), 0)
    col_ids = lax.broadcasted_iota(jnp.int32, (LANES, LANES), 1)
    eye = jnp.where(row_ids == col_ids, 1.0, 0.0).astype(jnp.float32)

    def step(block, carry):
        start = pl.multiple_of(block * LANES, LANES)
        rows = pl.ds(start, LANES)
        tile = work_ref[rows, rows]
        left = [tile[8 * g : 8 * g + 8, :] for g in range(groups)]
        right = [eye[8 * g : 8 * g + 8, :] for g in range(groups)]
        for k in range(LANES):
            g, s = k // 8, k % 8
            scale = lax.rsqrt(left[g][s : s + 1, k : k + 1])
            square = scale * scale
            left_row = left[g][s : s + 1, :] * square
            right_row = right[g][s : s + 1, :] * square
            diag_ref[k : k + 1, :] = right[g][s : s + 1, :] * scale
            for h in range(g if s < 7 else g + 1, groups):
                column = left[h][:, k : k + 1]
                left[h] = left[h] - column * left_row
                right[h] = right[h] - column * right_row
        inverse = diag_ref[...]
        work_ref[rows, pl.ds(pl.multiple_of(n + start, LANES), LANES)] = eye
        window = pl.ds(pl.multiple_of(start + LANES, LANES), n)
        solved = jnp.dot(inverse, work_ref[rows, window], precision=HIGHEST, preferred_element_type=jnp.float32)
        work_ref[rows, window] = solved

        def below(other, inner):
            other_rows = pl.ds(pl.multiple_of(other * LANES, LANES), LANES)
            lower = work_ref[rows, other_rows]
            work_ref[other_rows, window] = work_ref[other_rows, window] - lax.dot_general(
                lower,
                work_ref[rows, window],
                (((0,), (0,)), ((), ())),
                precision=HIGHEST,
                preferred_element_type=jnp.float32,
            )
            return inner

        lax.fori_loop(block + 1, count, below, 0)
        return carry

    lax.fori_loop(begin, end, step, 0)


def factor_call(kernel, operand, shape, scratch, flops):
    return pl.pallas_call(
        kernel,
        out_shape=jax.ShapeDtypeStruct(shape, jnp.float32),
        in_specs=[pl.BlockSpec(memory_space=pltpu.VMEM)],
        out_specs=pl.BlockSpec(memory_space=pltpu.VMEM),
        scratch_shapes=scratch + [pltpu.VMEM((LANES, LANES), jnp.float32)],
        compiler_params=pltpu.CompilerParams(vmem_limit_bytes=40 * 1024 * 1024),
        cost_estimate=pl.CostEstimate(flops=flops, bytes_accessed=4 * operand.size, transcendentals=0),
    )(operand)


def first_blocks(matrix, stop):
    n = matrix.shape[0]
    return factor_call(functools.partial(first_blocks_kernel, stop), matrix, (n, 2 * n), [], 95 * 10**9)


def last_blocks(state, start):
    n = state.shape[0]
    scratch = [pltpu.VMEM((n, 2 * n), jnp.float32)]
    return factor_call(functools.partial(last_blocks_kernel, start), state, (n, n), scratch, 25 * 10**9)


def trailing_kernel(
    chunk, place_ref, rows_ref, weights_ref, sums_ref, ridge_ref, pivots_ref, pivot_ridge_ref, pivot_ids_ref, cols_ref, out_ref
):
    width = cols_ref.shape[0]
    row_base = place_ref[0]
    row_group = place_ref[2]
    start = pl.program_id(0) * width
    group = start // row_group
    col_base = (place_ref[1] + group * place_ref[3]) * row_group + start - group * row_group
    cols = cols_ref[...]
    col_ids = col_base + lax.broadcasted_iota(jnp.int32, (1, width), 1)
    gram = lax.dot_general(pivots_ref[...], cols, (((1,), (1,)), ((), ())), preferred_element_type=jnp.float32)
    cross = gram * gram + jnp.where(pivot_ids_ref[...] == col_ids, pivot_ridge_ref[...], 0.0)
    centre = jnp.mean(cross, axis=0, keepdims=True)
    spread = (cross - centre).astype(jnp.bfloat16)
    for first in range(0, rows_ref.shape[0], chunk):
        part = pl.ds(first, chunk)
        gram = lax.dot_general(rows_ref[part, :], cols, (((1,), (1,)), ((), ())), preferred_element_type=jnp.float32)
        update = jnp.dot(weights_ref[part, :], spread, preferred_element_type=jnp.float32)
        row_ids = row_base + first + lax.broadcasted_iota(jnp.int32, (chunk, 1), 0)
        ridge = jnp.where(row_ids == col_ids, ridge_ref[part, :], 0.0)
        out_ref[part, :] = gram * gram + ridge - (update + sums_ref[part, :] * centre)


def trailing_update(place, rows, weights, sums, ridge, pivots, pivot_ridge, pivot_ids, cols):
    row_group, depth = rows.shape
    col_group = cols.shape[0]
    width = min(512, row_group)
    chunk = min(512, row_group)
    held = pl.BlockSpec(memory_space=pltpu.VMEM)
    return pl.pallas_call(
        functools.partial(trailing_kernel, chunk),
        out_shape=jax.ShapeDtypeStruct((row_group, col_group), jnp.float32),
        grid=(col_group // width,),
        in_specs=[pl.BlockSpec(memory_space=pltpu.SMEM)]
        + [held] * 7
        + [pl.BlockSpec((width, depth), lambda j: (j, 0))],
        out_specs=pl.BlockSpec((row_group, width), lambda j: (0, j)),
        compiler_params=pltpu.CompilerParams(
            dimension_semantics=("arbitrary",), vmem_limit_bytes=52 * 1024 * 1024
        ),
        cost_estimate=pl.CostEstimate(
            flops=4 * row_group * col_group * depth,
            bytes_accessed=4 * row_group * col_group + 2 * depth * (2 * row_group + col_group),
            transcendentals=0,
        ),
    )(place, rows, weights, sums, ridge, pivots, pivot_ridge, pivot_ids, cols)


def partner_pairs(count, shift):
    return [(i, i ^ shift) for i in range(count)]


def in_order(parts, index):
    result = jnp.zeros((len(parts),) + parts[0].shape, parts[0].dtype)
    for shift, part in enumerate(parts):
        result = lax.dynamic_update_slice(result, part[None], (index ^ shift,) + (0,) * part.ndim)
    return result


def body(spectra, projection, kernel_slot, env_image, image_atoms):
    grid_rows = lax.axis_size("row")
    grid_cols = lax.axis_size("col")
    devices = grid_rows * grid_cols
    per_device = spectra.shape[0]
    total_rows = per_device * devices
    depth = projection.shape[1]
    row_group = total_rows // grid_rows
    capacity = max(1, per_device // devices)
    share = NB // devices
    row_index = lax.axis_index("row")
    col_index = lax.axis_index("col")

    projected = jnp.dot(spectra, projection, preferred_element_type=jnp.float32)
    factor = lax.rsqrt(jnp.mean(projected * projected, axis=1, keepdims=True) + NORM_EPS) * depth ** (-0.5)
    unit_rows = (projected * factor).astype(jnp.bfloat16)

    image_ids = jnp.arange(image_atoms.shape[0], dtype=jnp.int32)
    atoms = jnp.sum(jnp.where(env_image[:, None] == image_ids[None, :], image_atoms[None, :], 0), axis=1)
    meta = jnp.stack([kernel_slot // DIGIT, kernel_slot % DIGIT, atoms], axis=1).astype(jnp.bfloat16)
    meta = jnp.pad(meta, ((0, 0), (0, LANES - meta.shape[1])))
    rows_out = jnp.concatenate([unit_rows, meta], axis=1)

    positions = jnp.arange(per_device, dtype=jnp.int32)
    before = positions[None, :] < positions[:, None]

    def rank_of(label):
        return jnp.sum(((label[:, None] == label[None, :]) & before).astype(jnp.int32), axis=1)

    starts = [j % grid_rows * row_group + j // grid_rows * NB for j in range(PANELS)]
    tile = kernel_slot // NB
    tile_rank = rank_of(tile)
    pivot_place = jnp.full((per_device,), -1, jnp.int32)
    for j, first in enumerate(starts):
        pivot_place = jnp.where(tile == first // NB, j * share + tile_rank, pivot_place)
    pivot_sent = pick(one_hot(PANELS * share, pivot_place), rows_out)
    pivot_all = lax.all_gather(pivot_sent, ("row", "col"), axis=0, tiled=True)
    pivot_slot = slots_of(pivot_all[:, depth:])
    pivot_order = jnp.full((PANELS * NB,), -1, jnp.int32)
    for j, first in enumerate(starts):
        pivot_order = jnp.where(pivot_slot // NB == first // NB, j * NB + pivot_slot - first, pivot_order)
    pivot_rows = pick(one_hot(PANELS * NB, pivot_order), pivot_all)
    pivots = pivot_rows[:, :depth]
    pivot_ridge = ATOM_RIDGE * pivot_rows[:, depth + 2].astype(jnp.float32)
    pivot_ids = jnp.concatenate([first + jnp.arange(NB, dtype=jnp.int32) for first in starts])
    pivot_gram = lax.dot_general(pivots, pivots, (((1,), (1,)), ((), ())), preferred_element_type=jnp.float32)
    pivot_matrix = pivot_gram * pivot_gram + jnp.where(
        pivot_ids[:, None] == pivot_ids[None, :], pivot_ridge[:, None], 0.0
    )

    block = kernel_slot // per_device
    rank = rank_of(block)
    row_place = block * (2 * capacity) + rank
    col_place = column_owner(block, grid_cols) * (2 * capacity) + capacity + rank
    ids = lax.broadcasted_iota(jnp.int32, (2 * per_device, per_device), 0)
    selector = ((ids == row_place[None, :]) | (ids == col_place[None, :])).astype(jnp.bfloat16)
    sent = pick(selector, rows_out)
    received = lax.all_to_all(sent, ("row", "col"), split_axis=0, concat_axis=0, tiled=True)
    received = received.reshape(devices, 2, capacity, rows_out.shape[1])
    for_rows = received[:, 0].reshape(per_device, -1)
    for_cols = received[:, 1].reshape(per_device, -1)
    row_selector = one_hot(per_device, slots_of(for_rows[:, depth:]) % per_device)
    col_selector = one_hot(per_device, slots_of(for_cols[:, depth:]) % per_device)
    own_rows = pick(row_selector, for_rows[:, :depth])
    own_cols = pick(col_selector, for_cols[:, :depth])
    own_meta = lax.dot_general(
        for_rows[:, depth:], row_selector, (((0,), (1,)), ((), ())), preferred_element_type=jnp.float32
    ).astype(jnp.bfloat16)
    own_meta = jnp.pad(own_meta[:META_ROWS], ((0, 0), (0, depth - per_device)))
    own_block = jnp.concatenate([own_rows, own_meta], axis=0)

    row_parts = [own_block] + [
        lax.ppermute(own_block, "col", partner_pairs(grid_cols, shift)) for shift in range(1, grid_cols)
    ]
    even_parts = [own_cols] + [
        lax.ppermute(own_cols, "row", partner_pairs(grid_rows, shift)) for shift in range(2, grid_rows, 2)
    ]
    split = PANELS * NB // LANES * 3 // 4
    state = first_blocks(pivot_matrix, split)
    state, row_parts, even_parts = lax.optimization_barrier((state, row_parts, even_parts))
    odd_parts = [lax.ppermute(part, "row", partner_pairs(grid_rows, 1)) for part in even_parts]
    inverse = last_blocks(state, split)
    inverse, odd_parts = lax.optimization_barrier((inverse, odd_parts))
    col_parts = [part for pair in zip(even_parts, odd_parts) for part in pair]
    cols = in_order(col_parts, row_index).reshape(grid_rows * per_device, depth)
    rows = in_order([part[:per_device] for part in row_parts], col_index).reshape(row_group, depth)
    atoms_row = in_order([part[per_device + 2, :per_device].astype(jnp.float32) for part in row_parts], col_index)
    ridge = ATOM_RIDGE * atoms_row.reshape(row_group)

    row_positions = jnp.arange(row_group, dtype=jnp.int32)
    row_ids = row_index * row_group + row_positions
    gram = lax.dot_general(rows, pivots, (((1,), (1,)), ((), ())), preferred_element_type=jnp.float32)
    cross = gram * gram + jnp.where(row_ids[:, None] == pivot_ids[None, :], pivot_ridge[None, :], 0.0)
    panels = lax.dot_general(cross, inverse, (((1,), (1,)), ((), ())), precision=HIGH, preferred_element_type=jnp.float32)
    row_tile = row_positions // NB * grid_rows + row_index
    panel_of = jnp.arange(PANELS * NB, dtype=jnp.int32) // NB
    panels = jnp.where(row_tile[:, None] >= panel_of[None, :], panels, 0.0)
    weights = jnp.dot(panels, inverse, precision=HIGH, preferred_element_type=jnp.float32)
    place = jnp.stack([row_index * row_group, col_index, jnp.int32(row_group), jnp.int32(grid_cols)]).astype(jnp.int32)
    trailing = trailing_update(
        place,
        rows,
        weights.astype(jnp.bfloat16),
        jnp.sum(weights, axis=1, keepdims=True),
        ridge[:, None],
        pivots,
        pivot_ridge[:, None],
        pivot_ids[:, None],
        cols,
    )
    return (panels, trailing)


def solution(mesh):
    in_specs = (P(("row", "col"), None), P(), P(("row", "col")), P(("row", "col")), P())
    out_specs = (P("row", None), P("row", "col"))
    return jax.shard_map(body, mesh=mesh, in_specs=in_specs, out_specs=out_specs, check_vma=False)
```
